512 devices in a mesh: prow: 32 (over y, x), pcol: 16 (over z, core).
Axes of the slice: x: 4, y: 8, z: 8, core: 2. Of those that a mesh axis runs over, the one named last changes fastest.
Arguments:
- trailing: float32 [40960, 8192], P('prow', 'pcol'), may hold values from -6 to 6
- l_panel: float32 [40960, 512], P('prow', 'pcol'), as said below
- pivots: int32 [512], replicated, may hold values from 512 to 40959, as said below
Outputs:
- updated: float32 [40960, 8192], P('prow', 'pcol')
The draws below stay inside these ranges and needn't reach their ends.
Inputs may be any that keep to these rules, and one draw needn't show every extreme that they name: `pivots`: all pivot rows are different and lie below the first 512 rows; at most 32 of them lie among the 1280 rows of one prow index, and exactly 32 among those of one prow index in every draw. `l_panel`: rows below the first 512 are dense; the first 512 rows are zero on and above the diagonal.
All inputs are finite; a program needn't handle non-finite values.
Results may differ from the reference program's by a relative error of at most 0.000059.
Values sent between devices are 32-bit elements; how exact they have to be, the bound alone decides.
No kernel may reach another device: no remote copies, remote signals or barrier semaphores. Data moves between devices by JAX's collectives and lax.ppermute only.
A program may use at most 64 MiB of HBM per device.

```python
import jax
import jax.numpy as jnp
from jax import lax

NB = 512
ROWS_DEV = 1280
M = 40960
NCOLS = 8192
CAP = 32


def draw_l_panel(key, part):
    key = jax.random.fold_in(key, 5)
    values = jax.random.normal(key, (M, NB), jnp.float32)
    rows = jnp.arange(M)[:, None]
    cols = jnp.arange(NB)[None, :]
    top_scale = jnp.where(cols < rows, 0.5 / NB ** 0.5, 0.0)
    scale = jnp.where(rows < NB, top_scale, 1.0 / NB ** 0.5)
    return (values * scale).astype(jnp.float32)


def draw_pivots(key, part):
    key = jax.random.fold_in(key, 11)
    key_hot, key_slot, key_score, key_order = jax.random.split(key, 4)
    owners = M // ROWS_DEV
    hot = jax.random.randint(key_hot, (), 0, owners)
    other = jax.random.permutation(key_slot, (owners - 1) * CAP)[:NB - CAP]
    other_owner = other // CAP
    other_owner = other_owner + (other_owner >= hot).astype(jnp.int32)
    owner = jnp.concatenate([jnp.full((CAP,), hot, jnp.int32), other_owner.astype(jnp.int32)])
    rank = jnp.concatenate([jnp.arange(CAP, dtype=jnp.int32), (other % CAP).astype(jnp.int32)])
    scores = jax.random.randint(key_score, (owners, ROWS_DEV), 0, 32768) * ROWS_DEV + jnp.arange(ROWS_DEV)[None, :]
    blocked = (jnp.arange(owners)[:, None] == 0) & (jnp.arange(ROWS_DEV)[None, :] < NB)
    scores = jnp.where(blocked, 32768 * ROWS_DEV + ROWS_DEV, scores)
    order = jnp.argsort(scores, axis=1)
    local = order[owner, rank]
    rows = owner * ROWS_DEV + local
    shuffle = jax.random.permutation(key_order, NB)
    return rows[shuffle].astype(jnp.int32)


def shard_levels(key, dims, cuts, least, high):
    def one(position, blocks):
        steps = jax.random.uniform(jax.random.fold_in(jax.random.fold_in(key, 6), position), (blocks,), jnp.float32, least / len(cuts), high / len(cuts))
        return jnp.repeat(jnp.exp(steps), dims[position] // blocks).reshape((-1,) + (1,) * (len(dims) - position - 1))

    gain = one(*cuts[0])
    for cut in cuts[1:]:
        gain = gain * one(*cut)
    return gain


def normal_values(stream_key, dims, deviation, limit, pieces=(), kind=jnp.bfloat16):
    entries = deviation * jax.random.normal(stream_key, dims, jnp.float32)
    if pieces:
        entries = entries * shard_levels(stream_key, dims, pieces, -0.22, 0.18)
    return jnp.clip(entries, -limit, limit).astype(kind)


def setup_inputs(seed: int = 0) -> dict:
    key_list = jax.random.split(jax.random.key(seed), 4)
    return {
        "trailing": normal_values(key_list[0], (M, NCOLS), 1.0, 6.0, ((0, 32), (1, 16)), jnp.float32),
        "l_panel": draw_l_panel(jax.random.fold_in(key_list[3], 71), 0),
        "pivots": draw_pivots(jax.random.fold_in(key_list[3], 71), 0),
    }


def reference(trailing, l_panel, pivots):
    top_orig = trailing[:NB]
    chosen = trailing[pivots]
    swapped = trailing.at[pivots].set(top_orig)
    upper = jax.scipy.linalg.solve_triangular(l_panel[:NB], chosen, lower=True, unit_diagonal=True)
    below = swapped[NB:] - jnp.dot(l_panel[NB:], upper, precision=lax.Precision.HIGHEST)
    return jnp.concatenate([upper, below], axis=0)
```

```python
import jax
import jax.numpy as jnp
from jax import lax
from jax.experimental import pallas as pl
from jax.experimental.pallas import tpu as pltpu
from jax.sharding import PartitionSpec as P

NX, NY = 4, 8
NPROW = NX * NY
CAP = 32
HI = lax.Precision.HIGHEST


def dot(a, b, dims=((1,), (0,)), precision=HI):
    return lax.dot_general(a, b, (dims, ((), ())), precision=precision, preferred_element_type=jnp.float32)


def split(a):
    hi = a.astype(jnp.bfloat16)
    lo = (a - hi.astype(jnp.float32)).astype(jnp.bfloat16)
    return hi, lo


def prep_kernel(lt_ref, hi_ref, lo_ref):
    hi, lo = split(lt_ref[...].T)
    hi_ref[...] = hi
    lo_ref[...] = lo


def prep(lt):
    k, rows = lt.shape
    tile = 256
    return pl.pallas_call(
        prep_kernel,
        grid=(rows // tile,),
        in_specs=[pl.BlockSpec((k, tile), lambda i: (0, i))],
        out_specs=[pl.BlockSpec((tile, k), lambda i: (i, 0))] * 2,
        out_shape=[jax.ShapeDtypeStruct((rows, k), jnp.bfloat16)] * 2,
        name="prep_l",
    )(lt)


def invert_upper(u_ref, m_ref):
    n = u_ref.shape[0]
    base = 128
    row = lax.broadcasted_iota(jnp.int32, (base, base), 0)
    col = lax.broadcasted_iota(jnp.int32, (base, base), 1)
    eye = jnp.where(row == col, 1.0, 0.0)
    blocks = [u_ref[pl.ds(b * base, base), pl.ds(b * base, base)] for b in range(n // base)]
    invs = [eye] * len(blocks)
    s = 1
    while s < base:
        mask = (row // (2 * s) == col // (2 * s)) & (row % (2 * s) < s) & (col % (2 * s) >= s)
        parts = [jnp.where(mask, u, 0.0) for u in blocks]
        if s == 1:
            invs = [m - q for m, q in zip(invs, parts)]
        else:
            half = [dot(m, q) for m, q in zip(invs, parts)]
            invs = [m - dot(h, m) for m, h in zip(invs, half)]
        s *= 2
    m_ref[...] = jnp.zeros_like(m_ref)
    for b, m in enumerate(invs):
        m_ref[pl.ds(b * base, base), pl.ds(b * base, base)] = m
    s = base
    while s < n:
        for b in range(0, n, 2 * s):
            up, dn = pl.ds(b, s), pl.ds(b + s, s)
            t = dot(m_ref[up, up], u_ref[up, dn])
            m_ref[up, dn] = -dot(t, m_ref[dn, dn])
        s *= 2


def update_kernel(rows_ref, first_ref, u_ref, chosen_ref, top_ref, hi_ref, lo_ref, trail_ref, out_ref, m_ref, x_ref):
    n = u_ref.shape[0]
    out_ref[...] = trail_ref[...]
    for r in range(CAP):
        row = rows_ref[r]

        @pl.when(row >= 0)
        def _(r=r, row=row):
            out_ref[pl.ds(row, 1), :] = top_ref[pl.ds(r, 1), :]

    invert_upper(u_ref, m_ref)
    x_ref[...] = dot(m_ref[...].T, chosen_ref[...])
    xhi, xlo = split(x_ref[...])
    tile = 256
    for i in range(out_ref.shape[0] // tile):
        here = pl.ds(i * tile, tile)
        hi, lo = hi_ref[here, :], lo_ref[here, :]
        acc = dot(hi, xhi, precision=None) + (dot(lo, xhi, precision=None) + dot(hi, xlo, precision=None))
        out_ref[here, :] = out_ref[here, :] - acc

    @pl.when(first_ref[0] == 1)
    def _():
        out_ref[pl.ds(0, n), :] = x_ref[...]


def update(rows, first, u, chosen, top, hi, lo, trailing):
    n = u.shape[0]
    smem = pl.BlockSpec(memory_space=pltpu.SMEM)
    vmem = pl.BlockSpec(memory_space=pltpu.VMEM)
    return pl.pallas_call(
        update_kernel,
        in_specs=[smem, smem] + [vmem] * 6,
        out_specs=vmem,
        out_shape=jax.ShapeDtypeStruct(trailing.shape, jnp.float32),
        scratch_shapes=[pltpu.VMEM((n, n), jnp.float32), pltpu.VMEM((n, trailing.shape[1]), jnp.float32)],
        compiler_params=pltpu.CompilerParams(vmem_limit_bytes=40 * 1024 * 1024),
        name="solve_update",
    )(rows, first, u, chosen, top, hi, lo, trailing)


def to_x(k):
    return [(0, k)]


def to_y(k):
    return [(x, NX * k + x) for x in range(NX)]


def on_device(trailing, l_panel, pivots):
    rows_here, cols_here = trailing.shape
    block = pivots.shape[0]
    p = lax.axis_index("prow")

    lt = l_panel.T
    lt_full = lax.all_gather(lt, "pcol", axis=0, tiled=True)

    slab = lt[:, :block]
    got = [lax.ppermute(slab, "prow", to_x(k)) for k in range(1, NX)]
    slab = jnp.where(p == 0, slab, sum(got))
    got = [lax.ppermute(slab, "prow", to_y(k)) for k in range(1, NY)]
    slab = jnp.where(p < NX, slab, sum(got))
    u = lax.all_gather(slab, "pcol", axis=0, tiled=True)

    owner = pivots // rows_here
    local = pivots % rows_here
    ks = jnp.arange(block, dtype=jnp.int32)
    before = (owner[None, :] == owner[:, None]) & (ks[None, :] < ks[:, None])
    slot = owner * CAP + jnp.sum(before.astype(jnp.int32), axis=1)
    mine = slot[None, :] == (p * CAP + jnp.arange(CAP, dtype=jnp.int32))[:, None]
    rows = jnp.sum(jnp.where(mine, local[None, :] + 1, 0), axis=1) - 1
    slots = jnp.arange(NPROW * CAP, dtype=jnp.int32)
    k_of = jnp.sum(jnp.where(slot[None, :] == slots[:, None], ks[None, :], 0), axis=1)

    picked = trailing.at[jnp.maximum(rows, 0)].get(mode="promise_in_bounds")
    sent = jnp.broadcast_to(picked[None], (NPROW, CAP, cols_here))
    every = lax.all_to_all(sent, "prow", 0, 0, tiled=True).reshape(NPROW * CAP, cols_here)
    chosen = every.at[slot].get(mode="promise_in_bounds")

    tops = trailing[:block].at[k_of].get(mode="promise_in_bounds")
    tops = tops.reshape(NY, NX, CAP, cols_here)
    got = [lax.ppermute(tops[:, k], "prow", to_x(k)) for k in range(1, NX)]
    tops = jnp.where(p == 0, tops[:, 0], sum(got))
    got = [lax.ppermute(tops[k], "prow", to_y(k)) for k in range(1, NY)]
    top = jnp.where(p < NX, tops[0], sum(got))

    hi, lo = prep(lt_full)
    first = (p == 0).astype(jnp.int32)[None]
    return update(rows, first, u, chosen, top, hi, lo, trailing)


def solution(mesh):
    placed = (P("prow", "pcol"), P("prow", "pcol"), P())
    return jax.shard_map(
        on_device, mesh=mesh, in_specs=placed, out_specs=P("prow", "pcol"), check_vma=False
    )
```

```python
import jax
import jax.numpy as jnp
from jax import lax
from jax.experimental import pallas as pl
from jax.experimental.pallas import tpu as pltpu
from jax.sharding import Mesh, PartitionSpec as P

NX, NY, NZ, NC = 4, 8, 8, 2
NPROW = NX * NY
CAP = 32
LANES = 128
SHARE = LANES // CAP
PROW, PCOL = ("y", "x"), ("z", "c")
HI = lax.Precision.HIGHEST
SMEM = pl.BlockSpec(memory_space=pltpu.SMEM)
VMEM = pl.BlockSpec(memory_space=pltpu.VMEM)


def dot(a, b, dims=((1,), (0,)), precision=HI):
    return lax.dot_general(a, b, (dims, ((), ())), precision=precision, preferred_element_type=jnp.float32)


def split(a):
    hi = a.astype(jnp.bfloat16)
    lo = (a - hi.astype(jnp.float32)).astype(jnp.bfloat16)
    return hi, lo


def pick_kernel(rows_ref, group_ref, trail_ref, out_ref, near, lanes, sems):
    def copy(r):
        tile = pl.multiple_of((jnp.maximum(rows_ref[r], 0) // 8) * 8, 8)
        return pltpu.make_async_copy(trail_ref.at[pl.ds(tile, 8), :], near.at[r], sems.at[r])

    for r in range(CAP):
        copy(r).start()
    lanes[...] = jnp.zeros_like(lanes)
    base = group_ref[0] * CAP
    for r in range(CAP):
        copy(r).wait()
        row = jnp.maximum(rows_ref[r], 0) % 8
        lanes[pl.ds(base + r, 1), :] = near[r, pl.ds(row, 1), :]
    out_ref[...] = lanes[...].T


def pick(rows, group, trailing):
    cols = trailing.shape[1]
    return pl.pallas_call(
        pick_kernel,
        in_specs=[SMEM, SMEM, pl.BlockSpec(memory_space=pl.ANY)],
        out_specs=VMEM,
        out_shape=jax.ShapeDtypeStruct((cols, LANES), jnp.float32),
        scratch_shapes=[
            pltpu.VMEM((CAP, 8, cols), jnp.float32),
            pltpu.VMEM((LANES, cols), jnp.float32),
            pltpu.SemaphoreType.DMA((CAP,)),
        ],
        name="pick_rows",
    )(rows, group, trailing)


def order_kernel(slots_ref, onehot_ref, out_ref):
    owners, cols, _ = slots_ref.shape
    acc = None
    for g in range(owners // SHARE):
        x, y = divmod(SHARE * g, NY)
        part = slots_ref[NX * y + x]
        for i in range(1, SHARE):
            part = part + slots_ref[NX * (y + i) + x]
        hi, rest = split(part)
        mid, lo = split(part - hi.astype(jnp.float32))
        three = jnp.concatenate([hi, mid, lo], axis=0)
        got = dot(three, onehot_ref[pl.ds(g * LANES, LANES), :], precision=None)
        acc = got if acc is None else acc + got
    rows = acc[:cols] + acc[cols : 2 * cols] + acc[2 * cols :]
    out_ref[...] = jnp.broadcast_to(rows[None], out_ref.shape)


def to_order(slots, onehot):
    owners, cols, _ = slots.shape
    return pl.pallas_call(
        order_kernel,
        in_specs=[VMEM, VMEM],
        out_specs=VMEM,
        out_shape=jax.ShapeDtypeStruct((owners, cols, onehot.shape[1]), jnp.float32),
        name="slots_to_order",
    )(slots, onehot)


def tops_kernel(first_ref, onehot_ref, trail_ref, *refs):
    outs, sems = refs[:NX], refs[NX]

    def run(pick, top, rows):
        n = top.shape[0]
        reads = [
            pltpu.make_async_copy(trail_ref.at[pl.ds(0, n), :], top, sems.at[0]),
            pltpu.make_async_copy(onehot_ref, pick, sems.at[1]),
        ]
        for copy in reads:
            copy.start()
        for copy in reads:
            copy.wait()
        hi, rest = split(top[...])
        mid, lo = split(top[...] - hi.astype(jnp.float32))
        writes = []
        for x in range(NX):
            here = pick[pl.ds(x * NY * CAP, NY * CAP), :]
            got = dot(here, hi, precision=None) + dot(here, mid, precision=None)
            rows[x] = got + dot(here, lo, precision=None)
            writes.append(pltpu.make_async_copy(rows.at[x], outs[x], sems.at[2 + x]))
            writes[-1].start()
        for copy in writes:
            copy.wait()

    @pl.when(first_ref[0] == 1)
    def _():
        slots, n = onehot_ref.shape
        cols = trail_ref.shape[1]
        pl.run_scoped(
            run,
            pltpu.VMEM((slots, n), jnp.bfloat16),
            pltpu.VMEM((n, cols), jnp.float32),
            pltpu.VMEM((NX, NY * CAP, cols), jnp.float32),
        )


def to_owners(first, onehot, trailing):
    cols = trailing.shape[1]
    hbm = pl.BlockSpec(memory_space=pl.ANY)
    return pl.pallas_call(
        tops_kernel,
        in_specs=[SMEM, hbm, hbm],
        out_specs=[hbm] * NX,
        out_shape=[jax.ShapeDtypeStruct((NY * CAP, cols), jnp.float32)] * NX,
        scratch_shapes=[pltpu.SemaphoreType.DMA((2 + NX,))],
        compiler_params=pltpu.CompilerParams(vmem_limit_bytes=24 * 1024 * 1024),
        name="tops_to_owners",
    )(first, onehot, trailing)


def invert_upper(u_ref, m_ref, between):
    n = u_ref.shape[0]
    base = 128
    row = lax.broadcasted_iota(jnp.int32, (base, base), 0)
    col = lax.broadcasted_iota(jnp.int32, (base, base), 1)
    eye = jnp.where(row == col, 1.0, 0.0)
    blocks = [u_ref[pl.ds(b * base, base), pl.ds(b * base, base)] for b in range(n // base)]
    invs = [eye] * len(blocks)
    m_ref[...] = jnp.zeros_like(m_ref)
    s = 1
    while s < base:
        mask = (row // (2 * s) == col // (2 * s)) & (row % (2 * s) < s) & (col % (2 * s) >= s)
        parts = [jnp.where(mask, u, 0.0) for u in blocks]
        if s == 1:
            invs = [m - q for m, q in zip(invs, parts)]
        else:
            half = [dot(m, q) for m, q in zip(invs, parts)]
            invs = [m - dot(h, m) for m, h in zip(invs, half)]
        between()
        s *= 2
    for b, m in enumerate(invs):
        m_ref[pl.ds(b * base, base), pl.ds(b * base, base)] = m
    s = base
    while s < n:
        for b in range(0, n, 2 * s):
            up, dn = pl.ds(b, s), pl.ds(b + s, s)
            t = dot(m_ref[up, up], u_ref[up, dn])
            m_ref[up, dn] = -dot(t, m_ref[dn, dn])
        s *= 2


TILE = 256


def factor_kernel(full_ref, m3_ref, l2_ref, u, m, lt, sems):
    n, rows = lt.shape
    get_u = pltpu.make_async_copy(full_ref.at[:, pl.ds(rows, n)], u, sems.at[0])
    get_l = pltpu.make_async_copy(full_ref.at[:, pl.ds(0, rows)], lt, sems.at[1])
    get_u.start()
    get_l.start()
    get_u.wait()

    todo = list(range(rows // TILE))

    def between():
        if not todo:
            return
        i = todo.pop(0)
        if i == 0:
            get_l.wait()
        at = pl.ds(i * TILE, TILE)
        hi, lo = split(lt[:, at].T)
        l2_ref[at, pl.ds(0, n)] = hi
        l2_ref[at, pl.ds(n, n)] = lo

    invert_upper(u, m, between)
    while todo:
        between()
    hi, lo = split(m[...])
    m3_ref[pl.ds(0, n), :] = hi
    m3_ref[pl.ds(n, n), :] = hi
    m3_ref[pl.ds(2 * n, n), :] = lo


def factor(full, rows):
    n = full.shape[0]
    f32, bf16 = jnp.float32, jnp.bfloat16
    return pl.pallas_call(
        factor_kernel,
        in_specs=[pl.BlockSpec(memory_space=pl.ANY)],
        out_specs=[VMEM, VMEM],
        out_shape=[jax.ShapeDtypeStruct((3 * n, n), bf16), jax.ShapeDtypeStruct((rows, 2 * n), bf16)],
        scratch_shapes=[
            pltpu.VMEM((n, n), f32),
            pltpu.VMEM((n, n), f32),
            pltpu.VMEM((n, rows), f32),
            pltpu.SemaphoreType.DMA((2,)),
        ],
        compiler_params=pltpu.CompilerParams(vmem_limit_bytes=56 * 1024 * 1024),
        name="factor",
    )(full)


def update_kernel(
    rows_ref, first_ref, top_ref, m3_ref, l2_ref, ct_ref, trail_ref, out_ref, m3, l2, ct, x3, here, sems
):
    rows, n = l2.shape[0], ct.shape[1]
    tiles, late = rows // TILE, n // TILE
    sources = ((ct_ref, ct), (m3_ref, m3), (trail_ref, here), (l2_ref, l2))
    gets = [pltpu.make_async_copy(a, b, sems.at[tiles + i]) for i, (a, b) in enumerate(sources)]
    for copy in gets:
        copy.start()
    gets[0].wait()
    gets[1].wait()
    hi, lo = split(ct[...])
    xt = dot(jnp.concatenate([hi, lo, hi], axis=1), m3[...], precision=None)
    hi, lo = split(xt)
    x3[:, pl.ds(0, n)] = hi
    x3[:, pl.ds(n, n)] = hi
    x3[:, pl.ds(2 * n, n)] = lo

    gets[2].wait()
    for r in range(CAP):
        row = rows_ref[r]

        @pl.when(row >= 0)
        def _(r=r, row=row):
            here[pl.ds(row, 1), :] = top_ref[pl.ds(r, 1), :]

    gets[3].wait()
    puts = []

    def put(i):
        at = pl.ds(i * TILE, TILE)
        puts.append(pltpu.make_async_copy(here.at[at, :], out_ref.at[at, :], sems.at[i]))
        puts[-1].start()

    both = ((1,), (1,))
    for i in list(range(late, tiles)) + list(range(late)):
        at = pl.ds(i * TILE, TILE)
        acc = dot(l2[at, :], x3[:, pl.ds(0, 2 * n)], both, None)
        acc = acc + dot(l2[at, pl.ds(0, n)], x3[:, pl.ds(2 * n, n)], both, None)
        here[at, :] = here[at, :] - acc
        if i >= late:
            put(i)

    @pl.when(first_ref[0] == 1)
    def _():
        here[pl.ds(0, n), :] = xt.T

    for i in range(late):
        put(i)
    for copy in puts:
        copy.wait()


def update(rows, first, top, m3, l2, ct, trailing):
    height, cols = trailing.shape
    n = ct.shape[1]
    hbm = pl.BlockSpec(memory_space=pl.ANY)
    f32, bf16 = jnp.float32, jnp.bfloat16
    return pl.pallas_call(
        update_kernel,
        in_specs=[SMEM, SMEM, VMEM, hbm, hbm, hbm, hbm],
        out_specs=hbm,
        out_shape=jax.ShapeDtypeStruct(trailing.shape, f32),
        scratch_shapes=[
            pltpu.VMEM(m3.shape, bf16),
            pltpu.VMEM(l2.shape, bf16),
            pltpu.VMEM(ct.shape, f32),
            pltpu.VMEM((cols, 3 * n), bf16),
            pltpu.VMEM((height, cols), f32),
            pltpu.SemaphoreType.DMA((height // TILE + 4,)),
        ],
        compiler_params=pltpu.CompilerParams(vmem_limit_bytes=56 * 1024 * 1024),
        name="solve_update",
    )(rows, first, top, m3, l2, ct, trailing)


def to_x(k):
    return [(0, k)]


def to_y(k):
    return [(x, NX * k + x) for x in range(NX)]


def after(value, *others):
    return lax.optimization_barrier((value, *others))[0]


def on_device(trailing, l_panel, pivots):
    rows_here, cols_here = trailing.shape
    block = pivots.shape[0]
    p = lax.axis_index(PROW)
    first = (p == 0).astype(jnp.int32)[None]

    owner = pivots // rows_here
    local = pivots % rows_here
    ks = jnp.arange(block, dtype=jnp.int32)
    before = (owner[None, :] == owner[:, None]) & (ks[None, :] < ks[:, None])
    place = (owner % NX) * NY + owner // NX
    slot = place * CAP + jnp.sum(before.astype(jnp.int32), axis=1)
    y, x = lax.axis_index("y"), lax.axis_index("x")
    mine = slot[None, :] == ((x * NY + y) * CAP + jnp.arange(CAP, dtype=jnp.int32))[:, None]
    rows = jnp.sum(jnp.where(mine, local[None, :] + 1, 0), axis=1) - 1
    slots = jnp.arange(NPROW * CAP, dtype=jnp.int32)
    onehot = (slot[None, :] == slots[:, None]).astype(jnp.bfloat16)
    lanes = pick(rows, (y % SHARE)[None], trailing)

    lt = l_panel.T
    slab = lt[:, :block]
    got = [lax.ppermute(slab, PROW, to_x(k)) for k in range(1, NX)]
    slab = jnp.where(p == 0, slab, sum(got))

    slab, lanes = lax.optimization_barrier((slab, lanes))

    got = [lax.ppermute(slab, PROW, to_y(k)) for k in range(1, NY)]
    lanes = after(lanes, got[0])
    slab = jnp.where(p < NX, slab, sum(got))

    full = lax.all_gather(jnp.concatenate([lt, slab], axis=1), PCOL, axis=0, tiled=True)

    share = lanes.reshape(NPROW, cols_here // NPROW, LANES)
    share = lax.all_to_all(share, PROW, 0, 0, tiled=True)

    tops = to_owners(first, onehot, after(trailing, slab))
    tops_x = [lax.ppermute(tops[k], PROW, to_x(k)) for k in range(1, NX)]

    ct = to_order(share, onehot)
    ct, tops_x = lax.optimization_barrier((ct, tops_x))
    ct = lax.all_to_all(ct, PROW, 0, 0, tiled=True).reshape(cols_here, block)

    tops = jnp.where(p == 0, tops[0], sum(tops_x)).reshape(NY, CAP, cols_here)
    early, late = range(1, NY - 2), range(NY - 2, NY)
    got = [lax.ppermute(tops[k], PROW, to_y(k)) for k in early]
    m3, l2 = factor(full, rows_here)
    tops, m3, got = lax.optimization_barrier((tops, m3, got))
    got += [lax.ppermute(tops[k], PROW, to_y(k)) for k in late]
    top = jnp.where(p < NX, tops[0], sum(got))
    return update(rows, first, top, m3, l2, ct, trailing)


def solution(mesh):
    grid = Mesh(mesh.devices.reshape(NY, NX, NZ, NC), ("y", "x", "z", "c"))
    placed = (P(PROW, PCOL), P(PROW, PCOL), P())
    return jax.shard_map(
        on_device, mesh=grid, in_specs=placed, out_specs=P(PROW, PCOL), check_vma=False
    )
```

```python
import jax
import jax.numpy as jnp
from jax import lax
from jax.experimental import pallas as pl
from jax.experimental.pallas import tpu as pltpu
from jax.sharding import Mesh, PartitionSpec as P

NX, NY, NZ, NC = 4, 8, 8, 2
NPROW = NX * NY
CAP = 32
LANES = 128
NEAR = 6
SHARE = LANES // CAP
PROW, PCOL = ("y", "x"), ("z", "c")
HI = lax.Precision.HIGHEST
SMEM = pl.BlockSpec(memory_space=pltpu.SMEM)
VMEM = pl.BlockSpec(memory_space=pltpu.VMEM)


def dot(a, b, dims=((1,), (0,)), precision=HI):
    return lax.dot_general(a, b, (dims, ((), ())), precision=precision, preferred_element_type=jnp.float32)


def split(a):
    hi = a.astype(jnp.bfloat16)
    lo = (a - hi.astype(jnp.float32)).astype(jnp.bfloat16)
    return hi, lo


def pick_kernel(rows_ref, group_ref, trail_ref, out_ref, near, lanes, sems):
    def copy(r):
        tile = pl.multiple_of((jnp.maximum(rows_ref[r], 0) // 8) * 8, 8)
        return pltpu.make_async_copy(trail_ref.at[pl.ds(tile, 8), :], near.at[r], sems.at[r])

    for r in range(CAP):
        copy(r).start()
    lanes[...] = jnp.zeros_like(lanes)
    base = group_ref[0] * CAP
    for r in range(CAP):
        copy(r).wait()
        row = jnp.maximum(rows_ref[r], 0) % 8
        lanes[pl.ds(base + r, 1), :] = near[r, pl.ds(row, 1), :]
    out_ref[...] = lanes[...].T


def pick(rows, group, trailing):
    cols = trailing.shape[1]
    return pl.pallas_call(
        pick_kernel,
        in_specs=[SMEM, SMEM, pl.BlockSpec(memory_space=pl.ANY)],
        out_specs=VMEM,
        out_shape=jax.ShapeDtypeStruct((cols, LANES), jnp.float32),
        scratch_shapes=[
            pltpu.VMEM((CAP, 8, cols), jnp.float32),
            pltpu.VMEM((LANES, cols), jnp.float32),
            pltpu.SemaphoreType.DMA((CAP,)),
        ],
        cost_estimate=pl.CostEstimate(flops=0, bytes_accessed=0, transcendentals=0),
        name="pick_rows",
    )(rows, group, trailing)


def onehot(slot, start, count):
    here = start + lax.broadcasted_iota(jnp.int32, (count, slot.shape[1]), 0)
    return jnp.where(here == slot, 1.0, 0.0).astype(jnp.bfloat16)


def pieces(a):
    hi, rest = split(a)
    mid, lo = split(a - hi.astype(jnp.float32))
    return hi, mid, lo


def owner_at(place):
    if place < NX * NEAR:
        x, y = divmod(place, NEAR)
    else:
        y, x = divmod(place, NX)
    return NX * y + x


def place_of(y, x):
    return jnp.where(y < NEAR, x * NEAR + y, NX * y + x)


def order_kernel(slot_ref, slots_ref, out_ref):
    owners, cols, _ = slots_ref.shape
    acc = None
    for g in range(owners // SHARE):
        part = slots_ref[owner_at(SHARE * g)]
        for i in range(1, SHARE):
            part = part + slots_ref[owner_at(SHARE * g + i)]
        three = jnp.concatenate(pieces(part), axis=0)
        got = dot(three, onehot(slot_ref[...], g * LANES, LANES), precision=None)
        acc = got if acc is None else acc + got
    rows = acc[:cols] + acc[cols : 2 * cols] + acc[2 * cols :]
    out_ref[...] = jnp.broadcast_to(rows[None], out_ref.shape)


def to_order(slots, slot):
    owners, cols, _ = slots.shape
    return pl.pallas_call(
        order_kernel,
        in_specs=[VMEM, VMEM],
        out_specs=VMEM,
        out_shape=jax.ShapeDtypeStruct((owners, cols, slot.shape[1]), jnp.float32),
        cost_estimate=pl.CostEstimate(flops=0, bytes_accessed=0, transcendentals=0),
        name="slots_to_order",
    )(slot, slots)


def tops_kernel(first_ref, slot_ref, trail_ref, *refs):
    outs, sem = refs[:-1], refs[-1]

    def run(top):
        read = pltpu.make_async_copy(trail_ref.at[pl.ds(0, top.shape[0]), :], top, sem)
        read.start()
        read.wait()
        parts = pieces(top[...])
        start = 0
        for out in outs:
            pick = onehot(slot_ref[...], start, out.shape[0])
            hi, mid, lo = (dot(pick, part, precision=None) for part in parts)
            out[...] = hi + mid + lo
            start += out.shape[0]

    @pl.when(first_ref[0] == 1)
    def _():
        pl.run_scoped(run, pltpu.VMEM((slot_ref.shape[1], trail_ref.shape[1]), jnp.float32))


def to_owners(first, slot, trailing):
    cols = trailing.shape[1]
    counts = [NEAR * CAP] * NX + [NX * CAP] * (NY - NEAR)
    return pl.pallas_call(
        tops_kernel,
        in_specs=[SMEM, VMEM, pl.BlockSpec(memory_space=pl.ANY)],
        out_specs=[VMEM] * len(counts),
        out_shape=[jax.ShapeDtypeStruct((count, cols), jnp.float32) for count in counts],
        scratch_shapes=[pltpu.SemaphoreType.DMA],
        compiler_params=pltpu.CompilerParams(vmem_limit_bytes=16 * 1024 * 1024),
        name="tops_to_owners",
    )(first, slot, trailing)


def invert_upper(u_ref, m_ref, between):
    n = u_ref.shape[0]
    base = 128
    row = lax.broadcasted_iota(jnp.int32, (base, base), 0)
    col = lax.broadcasted_iota(jnp.int32, (base, base), 1)
    eye = jnp.where(row == col, 1.0, 0.0)
    blocks = [u_ref[pl.ds(b * base, base), pl.ds(b * base, base)] for b in range(n // base)]
    invs = [eye] * len(blocks)
    m_ref[...] = jnp.zeros_like(m_ref)
    s = 1
    while s < base:
        mask = (row // (2 * s) == col // (2 * s)) & (row % (2 * s) < s) & (col % (2 * s) >= s)
        parts = [jnp.where(mask, u, 0.0) for u in blocks]
        if s == 1:
            invs = [m - q for m, q in zip(invs, parts)]
        else:
            half = [dot(m, q) for m, q in zip(invs, parts)]
            invs = [m - dot(h, m) for m, h in zip(invs, half)]
        between(s)
        s *= 2
    for b, m in enumerate(invs):
        m_ref[pl.ds(b * base, base), pl.ds(b * base, base)] = m
    s = base
    while s < n:
        for b in range(0, n, 2 * s):
            up, dn = pl.ds(b, s), pl.ds(b + s, s)
            t = dot(m_ref[up, up], u_ref[up, dn])
            m_ref[up, dn] = -dot(t, m_ref[dn, dn])
        s *= 2


TILE = 256


def factor_kernel(full_ref, m3_ref, l2_ref, u, m, lt, m3, l2, sems):
    n, rows = lt.shape
    get_u = pltpu.make_async_copy(full_ref.at[:, pl.ds(rows, n)], u, sems.at[0])
    get_l = pltpu.make_async_copy(full_ref.at[:, pl.ds(0, rows)], lt, sems.at[1])
    get_u.start()
    get_u.wait()
    get_l.start()

    todo = list(range(rows // TILE))
    puts = []

    def between(s):
        if s < 4 or not todo:
            return
        i = todo.pop(0)
        if i == 0:
            get_l.wait()
        at = pl.ds(i * TILE, TILE)
        hi, lo = split(lt[:, at].T)
        l2[at, pl.ds(0, n)] = hi
        l2[at, pl.ds(n, n)] = lo
        puts.append(pltpu.make_async_copy(l2.at[at, :], l2_ref.at[at, :], sems.at[2 + i]))
        puts[-1].start()

    invert_upper(u, m, between)
    while todo:
        between(n)
    hi, lo = split(m[...])
    m3[pl.ds(0, n), :] = hi
    m3[pl.ds(n, n), :] = hi
    m3[pl.ds(2 * n, n), :] = lo
    puts.append(pltpu.make_async_copy(m3, m3_ref, sems.at[2 + rows // TILE]))
    puts[-1].start()
    for copy in puts:
        copy.wait()


def factor(full, rows):
    n = full.shape[0]
    f32, bf16 = jnp.float32, jnp.bfloat16
    hbm = pl.BlockSpec(memory_space=pl.ANY)
    return pl.pallas_call(
        factor_kernel,
        in_specs=[hbm],
        out_specs=[hbm, hbm],
        out_shape=[jax.ShapeDtypeStruct((3 * n, n), bf16), jax.ShapeDtypeStruct((rows, 2 * n), bf16)],
        scratch_shapes=[
            pltpu.VMEM((n, n), f32),
            pltpu.VMEM((n, n), f32),
            pltpu.VMEM((n, rows), f32),
            pltpu.VMEM((3 * n, n), bf16),
            pltpu.VMEM((rows, 2 * n), bf16),
            pltpu.SemaphoreType.DMA((3 + rows // TILE,)),
        ],
        compiler_params=pltpu.CompilerParams(vmem_limit_bytes=56 * 1024 * 1024),
        cost_estimate=pl.CostEstimate(flops=200_000_000_000, bytes_accessed=0, transcendentals=0),
        name="factor",
    )(full)


def update_kernel(
    rows_ref, first_ref, top_ref, m3_ref, l2_ref, ct_ref, trail_ref, out_ref, m3, l2, ct, x3, here, sems
):
    rows, n = l2.shape[0], ct.shape[1]
    tiles, late = rows // TILE, n // TILE
    sources = ((ct_ref, ct), (m3_ref, m3), (trail_ref, here), (l2_ref, l2))
    gets = [pltpu.make_async_copy(a, b, sems.at[tiles + i]) for i, (a, b) in enumerate(sources)]
    for copy in gets:
        copy.start()
    gets[0].wait()
    gets[1].wait()
    hi, lo = split(ct[...])
    xt = dot(jnp.concatenate([hi, lo, hi], axis=1), m3[...], precision=None)
    hi, lo = split(xt)
    x3[:, pl.ds(0, n)] = hi
    x3[:, pl.ds(n, n)] = hi
    x3[:, pl.ds(2 * n, n)] = lo

    gets[2].wait()
    for r in range(CAP):
        row = rows_ref[r]

        @pl.when(row >= 0)
        def _(r=r, row=row):
            here[pl.ds(row, 1), :] = top_ref[pl.ds(r, 1), :]

    gets[3].wait()
    puts = []

    def put(i):
        at = pl.ds(i * TILE, TILE)
        puts.append(pltpu.make_async_copy(here.at[at, :], out_ref.at[at, :], sems.at[i]))
        puts[-1].start()

    both = ((1,), (1,))
    for i in list(range(late, tiles)) + list(range(late)):
        at = pl.ds(i * TILE, TILE)
        acc = dot(l2[at, :], x3[:, pl.ds(0, 2 * n)], both, None)
        acc = acc + dot(l2[at, pl.ds(0, n)], x3[:, pl.ds(2 * n, n)], both, None)
        here[at, :] = here[at, :] - acc
        if i >= late:
            put(i)

    @pl.when(first_ref[0] == 1)
    def _():
        here[pl.ds(0, n), :] = xt.T

    for i in range(late):
        put(i)
    for copy in puts:
        copy.wait()


def update(rows, first, top, m3, l2, ct, trailing):
    height, cols = trailing.shape
    n = ct.shape[1]
    hbm = pl.BlockSpec(memory_space=pl.ANY)
    f32, bf16 = jnp.float32, jnp.bfloat16
    return pl.pallas_call(
        update_kernel,
        in_specs=[SMEM, SMEM, VMEM, hbm, hbm, hbm, hbm],
        out_specs=hbm,
        out_shape=jax.ShapeDtypeStruct(trailing.shape, f32),
        scratch_shapes=[
            pltpu.VMEM(m3.shape, bf16),
            pltpu.VMEM(l2.shape, bf16),
            pltpu.VMEM(ct.shape, f32),
            pltpu.VMEM((cols, 3 * n), bf16),
            pltpu.VMEM((height, cols), f32),
            pltpu.SemaphoreType.DMA((height // TILE + 4,)),
        ],
        compiler_params=pltpu.CompilerParams(vmem_limit_bytes=56 * 1024 * 1024),
        name="solve_update",
    )(rows, first, top, m3, l2, ct, trailing)


def to_x(k):
    return [(0, k)]


def to_y(k):
    return [(x, NX * k + x) for x in range(NX)]


def after(value, *others):
    return lax.optimization_barrier((value, *others))[0]


def on_device(trailing, l_panel, pivots):
    rows_here, cols_here = trailing.shape
    block = pivots.shape[0]
    p = lax.axis_index(PROW)
    first = (p == 0).astype(jnp.int32)[None]

    owner = pivots // rows_here
    local = pivots % rows_here
    ks = jnp.arange(block, dtype=jnp.int32)
    before = (owner[None, :] == owner[:, None]) & (ks[None, :] < ks[:, None])
    place = place_of(owner // NX, owner % NX)
    slot = place * CAP + jnp.sum(before.astype(jnp.int32), axis=1)
    y, x = lax.axis_index("y"), lax.axis_index("x")
    here = place_of(y, x)
    mine = slot[None, :] == (here * CAP + jnp.arange(CAP, dtype=jnp.int32))[:, None]
    rows = jnp.sum(jnp.where(mine, local[None, :] + 1, 0), axis=1) - 1
    lanes = pick(rows, (here % SHARE)[None], trailing)

    lt = l_panel.T
    slab = lt[:, :block]
    got = [lax.ppermute(slab, PROW, to_x(k)) for k in range(1, NX)]
    slab = jnp.where(p == 0, slab, sum(got))
    slab, lanes = lax.optimization_barrier((slab, lanes))
    got = [lax.ppermute(slab, PROW, to_y(k)) for k in range(1, NY)]
    slab = jnp.where(p < NX, slab, sum(got))

    full = lax.all_gather(jnp.concatenate([lt, slab], axis=1), PCOL, axis=0, tiled=True)

    tops = to_owners(first, slot[None, :], after(trailing, slab))
    near = [lax.ppermute(tops[k], PROW, to_x(k)) for k in range(1, NX)]
    far = [lax.ppermute(tops[NX + i], PROW, [(0, NX * (NEAR + i))]) for i in range(NY - NEAR)]

    lanes = after(lanes, tops[1])
    share = lanes.reshape(NPROW, cols_here // NPROW, LANES)
    share = lax.all_to_all(share, PROW, 0, 0, tiled=True)

    ct = to_order(share, slot[None, :])
    near, far = lax.optimization_barrier((near, far, ct))[:2]
    ct = lax.all_to_all(ct, PROW, 0, 0, tiled=True).reshape(cols_here, block)

    near = jnp.where(p == 0, tops[0], sum(near)).reshape(NEAR, CAP, cols_here)
    far = sum(far).reshape(NX, CAP, cols_here)
    got = []
    for k in range(1, NEAR):
        pairs = to_y(k)
        sent = near[k]
        if k < NX:
            pairs = pairs + [(NX * i, NX * i + k) for i in range(NEAR, NY)]
            sent = jnp.where(y == 0, near[k], far[k])
        got.append(lax.ppermute(sent, PROW, pairs))
    m3, l2 = factor(full, rows_here)
    got, m3 = lax.optimization_barrier((got, m3))
    own = jnp.where(y == 0, near[0], far[0])
    top = jnp.where((y == 0) | ((y >= NEAR) & (x == 0)), own, sum(got))

    return update(rows, first, top, m3, l2, ct, trailing)


def solution(mesh):
    grid = Mesh(mesh.devices.reshape(NY, NX, NZ, NC), ("y", "x", "z", "c"))
    placed = (P(PROW, PCOL), P(PROW, PCOL), P())
    return jax.shard_map(
        on_device, mesh=grid, in_specs=placed, out_specs=P(PROW, PCOL), check_vma=False
    )
```

```python
import jax
import jax.numpy as jnp
from jax import lax
from jax.experimental import pallas as pl
from jax.experimental.pallas import tpu as pltpu
from jax.sharding import Mesh, PartitionSpec as P

NX, NY, NZ, NC = 4, 8, 8, 2
NPROW = NX * NY
CAP = 32
LANES = 128
NEAR = 6
SHARE = LANES // CAP
PROW, PCOL = ("y", "x"), ("z", "c")
HI = lax.Precision.HIGHEST
SMEM = pl.BlockSpec(memory_space=pltpu.SMEM)
VMEM = pl.BlockSpec(memory_space=pltpu.VMEM)


def dot(a, b, dims=((1,), (0,)), precision=HI):
    return lax.dot_general(a, b, (dims, ((), ())), precision=precision, preferred_element_type=jnp.float32)


def split(a):
    hi = a.astype(jnp.bfloat16)
    lo = (a - hi.astype(jnp.float32)).astype(jnp.bfloat16)
    return hi, lo


def pick_kernel(rows_ref, group_ref, trail_ref, out_ref, near, lanes, sems):
    def copy(r):
        tile = pl.multiple_of((jnp.maximum(rows_ref[r], 0) // 8) * 8, 8)
        return pltpu.make_async_copy(trail_ref.at[pl.ds(tile, 8), :], near.at[r], sems.at[r])

    for r in range(CAP):
        copy(r).start()
    lanes[...] = jnp.zeros_like(lanes)
    base = group_ref[0] * CAP
    for r in range(CAP):
        copy(r).wait()
        row = jnp.maximum(rows_ref[r], 0) % 8
        lanes[pl.ds(base + r, 1), :] = near[r, pl.ds(row, 1), :]
    out_ref[...] = lanes[...].T


def pick(rows, group, trailing):
    cols = trailing.shape[1]
    return pl.pallas_call(
        pick_kernel,
        in_specs=[SMEM, SMEM, pl.BlockSpec(memory_space=pl.ANY)],
        out_specs=VMEM,
        out_shape=jax.ShapeDtypeStruct((cols, LANES), jnp.float32),
        scratch_shapes=[
            pltpu.VMEM((CAP, 8, cols), jnp.float32),
            pltpu.VMEM((LANES, cols), jnp.float32),
            pltpu.SemaphoreType.DMA((CAP,)),
        ],
        cost_estimate=pl.CostEstimate(flops=0, bytes_accessed=0, transcendentals=0),
        name="pick_rows",
    )(rows, group, trailing)


def onehot(slot, start, count):
    here = start + lax.broadcasted_iota(jnp.int32, (count, slot.shape[1]), 0)
    return jnp.where(here == slot, 1.0, 0.0).astype(jnp.bfloat16)


def pieces(a):
    hi, rest = split(a)
    mid, lo = split(a - hi.astype(jnp.float32))
    return hi, mid, lo


def owner_at(place):
    if place < NX * NEAR:
        x, y = divmod(place, NEAR)
    else:
        y, x = divmod(place, NX)
    return NX * y + x


def place_of(y, x):
    return jnp.where(y < NEAR, x * NEAR + y, NX * y + x)


def order_kernel(slot_ref, slots_ref, out_ref):
    owners, cols, _ = slots_ref.shape
    acc = None
    for g in range(owners // SHARE):
        part = slots_ref[owner_at(SHARE * g)]
        for i in range(1, SHARE):
            part = part + slots_ref[owner_at(SHARE * g + i)]
        three = jnp.concatenate(pieces(part), axis=0)
        got = dot(three, onehot(slot_ref[...], g * LANES, LANES), precision=None)
        acc = got if acc is None else acc + got
    rows = acc[:cols] + acc[cols : 2 * cols] + acc[2 * cols :]
    out_ref[...] = jnp.broadcast_to(rows[None], out_ref.shape)


def to_order(slots, slot):
    owners, cols, _ = slots.shape
    return pl.pallas_call(
        order_kernel,
        in_specs=[VMEM, VMEM],
        out_specs=VMEM,
        out_shape=jax.ShapeDtypeStruct((owners, cols, slot.shape[1]), jnp.float32),
        cost_estimate=pl.CostEstimate(flops=0, bytes_accessed=0, transcendentals=0),
        name="slots_to_order",
    )(slot, slots)


def tops_kernel(first_ref, slot_ref, trail_ref, *refs):
    blocks = NX + NY - NEAR
    outs, sems = refs[:blocks], refs[blocks]

    def run(top, rows):
        read = pltpu.make_async_copy(trail_ref.at[pl.ds(0, top.shape[0]), :], top, sems.at[blocks])
        read.start()
        read.wait()
        parts = pieces(top[...])
        writes = []
        start = 0
        for b, out in enumerate(outs):
            count = out.shape[0]
            pick = onehot(slot_ref[...], start, count)
            hi, mid, lo = (dot(pick, part, precision=None) for part in parts)
            rows[pl.ds(start, count), :] = hi + mid + lo
            writes.append(pltpu.make_async_copy(rows.at[pl.ds(start, count), :], out, sems.at[b]))
            writes[-1].start()
            start += count
        for copy in writes:
            copy.wait()

    @pl.when(first_ref[0] == 1)
    def _():
        n, cols = slot_ref.shape[1], trail_ref.shape[1]
        pl.run_scoped(
            run,
            pltpu.VMEM((n, cols), jnp.float32),
            pltpu.VMEM((NPROW * CAP, cols), jnp.float32),
        )


def to_owners(first, slot, trailing):
    cols = trailing.shape[1]
    hbm = pl.BlockSpec(memory_space=pltpu.HBM)
    counts = [NEAR * CAP] * NX + [NX * CAP] * (NY - NEAR)
    return pl.pallas_call(
        tops_kernel,
        in_specs=[SMEM, VMEM, pl.BlockSpec(memory_space=pl.ANY)],
        out_specs=[hbm] * len(counts),
        out_shape=[pltpu.HBM((count, cols), jnp.float32) for count in counts],
        scratch_shapes=[pltpu.SemaphoreType.DMA((len(counts) + 1,))],
        compiler_params=pltpu.CompilerParams(vmem_limit_bytes=24 * 1024 * 1024),
        cost_estimate=pl.CostEstimate(flops=20_000_000_000, bytes_accessed=0, transcendentals=0),
        name="tops_to_owners",
    )(first, slot, trailing)


def invert_upper(u_ref, m_ref, between):
    n = u_ref.shape[0]
    base = 128
    row = lax.broadcasted_iota(jnp.int32, (base, base), 0)
    col = lax.broadcasted_iota(jnp.int32, (base, base), 1)
    eye = jnp.where(row == col, 1.0, 0.0)
    blocks = [u_ref[pl.ds(b * base, base), pl.ds(b * base, base)] for b in range(n // base)]
    invs = [eye] * len(blocks)
    m_ref[...] = jnp.zeros_like(m_ref)
    s = 1
    while s < base:
        mask = (row // (2 * s) == col // (2 * s)) & (row % (2 * s) < s) & (col % (2 * s) >= s)
        parts = [jnp.where(mask, u, 0.0) for u in blocks]
        if s == 1:
            invs = [m - q for m, q in zip(invs, parts)]
        else:
            half = [dot(m, q) for m, q in zip(invs, parts)]
            invs = [m - dot(h, m) for m, h in zip(invs, half)]
        between(s)
        s *= 2
    for b, m in enumerate(invs):
        m_ref[pl.ds(b * base, base), pl.ds(b * base, base)] = m
    s = base
    while s < n:
        for b in range(0, n, 2 * s):
            up, dn = pl.ds(b, s), pl.ds(b + s, s)
            t = dot(m_ref[up, up], u_ref[up, dn])
            m_ref[up, dn] = -dot(t, m_ref[dn, dn])
        s *= 2


TILE = 256


def factor_kernel(full_ref, m3_ref, l2_ref, u, m, lt, m3, l2, sems):
    n, rows = lt.shape
    get_u = pltpu.make_async_copy(full_ref.at[:, pl.ds(rows, n)], u, sems.at[0])
    get_l = pltpu.make_async_copy(full_ref.at[:, pl.ds(0, rows)], lt, sems.at[1])
    get_u.start()
    get_u.wait()
    get_l.start()

    todo = list(range(rows // TILE))
    puts = []

    def between(s):
        if s < 4 or not todo:
            return
        i = todo.pop(0)
        if i == 0:
            get_l.wait()
        at = pl.ds(i * TILE, TILE)
        hi, lo = split(lt[:, at].T)
        l2[at, pl.ds(0, n)] = hi
        l2[at, pl.ds(n, n)] = lo
        puts.append(pltpu.make_async_copy(l2.at[at, :], l2_ref.at[at, :], sems.at[2 + i]))
        puts[-1].start()

    invert_upper(u, m, between)
    while todo:
        between(n)
    hi, lo = split(m[...])
    m3[pl.ds(0, n), :] = hi
    m3[pl.ds(n, n), :] = hi
    m3[pl.ds(2 * n, n), :] = lo
    puts.append(pltpu.make_async_copy(m3, m3_ref, sems.at[2 + rows // TILE]))
    puts[-1].start()
    for copy in puts:
        copy.wait()


def factor(full, rows):
    n = full.shape[0]
    f32, bf16 = jnp.float32, jnp.bfloat16
    hbm = pl.BlockSpec(memory_space=pl.ANY)
    return pl.pallas_call(
        factor_kernel,
        in_specs=[hbm],
        out_specs=[hbm, hbm],
        out_shape=[jax.ShapeDtypeStruct((3 * n, n), bf16), jax.ShapeDtypeStruct((rows, 2 * n), bf16)],
        scratch_shapes=[
            pltpu.VMEM((n, n), f32),
            pltpu.VMEM((n, n), f32),
            pltpu.VMEM((n, rows), f32),
            pltpu.VMEM((3 * n, n), bf16),
            pltpu.VMEM((rows, 2 * n), bf16),
            pltpu.SemaphoreType.DMA((3 + rows // TILE,)),
        ],
        compiler_params=pltpu.CompilerParams(vmem_limit_bytes=56 * 1024 * 1024),
        cost_estimate=pl.CostEstimate(flops=200_000_000_000, bytes_accessed=0, transcendentals=0),
        name="factor",
    )(full)


def update_kernel(rows_ref, flags_ref, *refs):
    parts, refs = refs[:NEAR], refs[NEAR:]
    m3_ref, l2_ref, ct_ref, trail_ref, out_ref, m3, l2, ct, x3, here, top, sems = refs
    rows, n = l2.shape[0], ct.shape[1]
    tiles, late = rows // TILE, n // TILE
    sources = ((ct_ref, ct), (m3_ref, m3), (trail_ref, here), (l2_ref, l2))
    gets = [pltpu.make_async_copy(a, b, sems.at[tiles + i]) for i, (a, b) in enumerate(sources)]
    for copy in gets:
        copy.start()
    received = parts[1][...]
    for part in parts[2:]:
        received = received + part[...]
    top[...] = jnp.where(flags_ref[1] == 1, parts[0][...], received)
    gets[0].wait()
    gets[1].wait()
    hi, lo = split(ct[...])
    xt = dot(jnp.concatenate([hi, lo, hi], axis=1), m3[...], precision=None)
    hi, lo = split(xt)
    x3[:, pl.ds(0, n)] = hi
    x3[:, pl.ds(n, n)] = hi
    x3[:, pl.ds(2 * n, n)] = lo

    gets[2].wait()
    for r in range(CAP):
        row = rows_ref[r]

        @pl.when(row >= 0)
        def _(r=r, row=row):
            here[pl.ds(row, 1), :] = top[pl.ds(r, 1), :]

    gets[3].wait()
    puts = []

    def put(i):
        at = pl.ds(i * TILE, TILE)
        puts.append(pltpu.make_async_copy(here.at[at, :], out_ref.at[at, :], sems.at[i]))
        puts[-1].start()

    both = ((1,), (1,))
    for i in list(range(late, tiles)) + list(range(late)):
        at = pl.ds(i * TILE, TILE)
        acc = dot(l2[at, :], x3[:, pl.ds(0, 2 * n)], both, None)
        acc = acc + dot(l2[at, pl.ds(0, n)], x3[:, pl.ds(2 * n, n)], both, None)
        here[at, :] = here[at, :] - acc
        if i >= late:
            put(i)

    @pl.when(flags_ref[0] == 1)
    def _():
        here[pl.ds(0, n), :] = xt.T

    for i in range(late):
        put(i)
    for copy in puts:
        copy.wait()


def update(rows, flags, parts, m3, l2, ct, trailing):
    height, cols = trailing.shape
    n = ct.shape[1]
    hbm = pl.BlockSpec(memory_space=pl.ANY)
    f32, bf16 = jnp.float32, jnp.bfloat16
    return pl.pallas_call(
        update_kernel,
        in_specs=[SMEM, SMEM] + [VMEM] * len(parts) + [hbm] * 4,
        out_specs=hbm,
        out_shape=jax.ShapeDtypeStruct(trailing.shape, f32),
        scratch_shapes=[
            pltpu.VMEM(m3.shape, bf16),
            pltpu.VMEM(l2.shape, bf16),
            pltpu.VMEM(ct.shape, f32),
            pltpu.VMEM((cols, 3 * n), bf16),
            pltpu.VMEM((height, cols), f32),
            pltpu.VMEM((CAP, cols), f32),
            pltpu.SemaphoreType.DMA((height // TILE + 4,)),
        ],
        compiler_params=pltpu.CompilerParams(vmem_limit_bytes=56 * 1024 * 1024),
        name="solve_update",
    )(rows, flags, *parts, m3, l2, ct, trailing)


def from_hubs(k):
    pairs = [(x, NX * k + x) for x in range(NX)]
    if k < NX:
        pairs += [(NX * y, NX * y + k) for y in range(NEAR, NY)]
    return pairs


def after(value, *others):
    return lax.optimization_barrier((value, *others))[0]


def on_device(trailing, l_panel, pivots):
    rows_here, cols_here = trailing.shape
    block = pivots.shape[0]
    p = lax.axis_index(PROW)
    first = (p == 0).astype(jnp.int32)[None]

    owner = pivots // rows_here
    local = pivots % rows_here
    ks = jnp.arange(block, dtype=jnp.int32)
    before = (owner[None, :] == owner[:, None]) & (ks[None, :] < ks[:, None])
    place = place_of(owner // NX, owner % NX)
    slot = place * CAP + jnp.sum(before.astype(jnp.int32), axis=1)
    y, x = lax.axis_index("y"), lax.axis_index("x")
    here = place_of(y, x)
    mine = slot[None, :] == (here * CAP + jnp.arange(CAP, dtype=jnp.int32))[:, None]
    rows = jnp.sum(jnp.where(mine, local[None, :] + 1, 0), axis=1) - 1
    hub = (y == 0) | ((y >= NEAR) & (x == 0))

    lt = l_panel.T
    slab = lt[:, :block]
    got = [lax.ppermute(slab, PROW, [(0, k)]) for k in range(1, NX)]
    slab = jnp.where(p == 0, slab, sum(got))
    lanes = pick(rows, (here % SHARE)[None], trailing)
    slab, lanes = lax.optimization_barrier((slab, lanes))
    got = [lax.ppermute(slab, PROW, [(x0, NX * k + x0) for x0 in range(NX)]) for k in range(1, NY)]
    slab = jnp.where(y == 0, slab, sum(got))

    tops = to_owners(first, slot[None, :], after(trailing, lanes))
    slab = after(slab, tops[1])

    full = lax.all_gather(jnp.concatenate([lt, slab], axis=1), PCOL, axis=0, tiled=True)

    near = [lax.ppermute(tops[k], PROW, [(0, k)]) for k in range(1, NX)]
    far = [lax.ppermute(tops[NX + i], PROW, [(0, NX * (NEAR + i))]) for i in range(NY - NEAR)]

    lanes = after(lanes, tops[1])
    share = lanes.reshape(NPROW, cols_here // NPROW, LANES)
    share = lax.all_to_all(share, PROW, 0, 0, tiled=True)

    ct = to_order(share, slot[None, :])
    near, far = lax.optimization_barrier((near, far, ct))[:2]
    ct = lax.all_to_all(ct, PROW, 0, 0, tiled=True).reshape(cols_here, block)

    near = jnp.where(p == 0, tops[0], sum(near)).reshape(NEAR, CAP, cols_here)
    far = sum(far).reshape(NX, CAP, cols_here)
    got = []
    for k in range(1, NEAR):
        sent = jnp.where(y == 0, near[k], far[k]) if k < NX else near[k]
        got.append(lax.ppermute(sent, PROW, from_hubs(k)))

    m3, l2 = factor(full, rows_here)
    got, m3 = lax.optimization_barrier((got, m3))
    own = jnp.where(y == 0, near[0], far[0])
    flags = jnp.stack([first[0], hub.astype(jnp.int32)])
    return update(rows, flags, [own] + got, m3, l2, ct, trailing)


def solution(mesh):
    grid = Mesh(mesh.devices.reshape(NY, NX, NZ, NC), ("y", "x", "z", "c"))
    placed = (P(PROW, PCOL), P(PROW, PCOL), P())
    return jax.shard_map(
        on_device, mesh=grid, in_specs=placed, out_specs=P(PROW, PCOL), check_vma=False
    )
```

```python
import jax
import jax.numpy as jnp
from jax import lax
from jax.experimental import pallas as pl
from jax.experimental.pallas import tpu as pltpu
from jax.sharding import Mesh, PartitionSpec as P

NX, NY, NZ, NC = 4, 8, 8, 2
NPROW = NX * NY
CAP = 32
LANES = 128
NEAR = 6
SHARE = LANES // CAP
PROW, PCOL = ("y", "x"), ("z", "c")
HI = lax.Precision.HIGHEST
SMEM = pl.BlockSpec(memory_space=pltpu.SMEM)
VMEM = pl.BlockSpec(memory_space=pltpu.VMEM)


def dot(a, b, dims=((1,), (0,)), precision=HI):
    return lax.dot_general(a, b, (dims, ((), ())), precision=precision, preferred_element_type=jnp.float32)


def split(a):
    hi = a.astype(jnp.bfloat16)
    lo = (a - hi.astype(jnp.float32)).astype(jnp.bfloat16)
    return hi, lo


def pick_kernel(rows_ref, group_ref, trail_ref, out_ref, near, lanes, sems):
    def copy(r):
        tile = pl.multiple_of((jnp.maximum(rows_ref[r], 0) // 8) * 8, 8)
        return pltpu.make_async_copy(trail_ref.at[pl.ds(tile, 8), :], near.at[r], sems.at[r])

    for r in range(CAP):
        copy(r).start()
    lanes[...] = jnp.zeros_like(lanes)
    base = group_ref[0] * CAP
    for r in range(CAP):
        copy(r).wait()
        row = jnp.maximum(rows_ref[r], 0) % 8
        lanes[pl.ds(base + r, 1), :] = near[r, pl.ds(row, 1), :]
    out_ref[...] = lanes[...].T


def pick(rows, group, trailing):
    cols = trailing.shape[1]
    return pl.pallas_call(
        pick_kernel,
        in_specs=[SMEM, SMEM, pl.BlockSpec(memory_space=pl.ANY)],
        out_specs=VMEM,
        out_shape=jax.ShapeDtypeStruct((cols, LANES), jnp.float32),
        scratch_shapes=[
            pltpu.VMEM((CAP, 8, cols), jnp.float32),
            pltpu.VMEM((LANES, cols), jnp.float32),
            pltpu.SemaphoreType.DMA((CAP,)),
        ],
        cost_estimate=pl.CostEstimate(flops=0, bytes_accessed=0, transcendentals=0),
        name="pick_rows",
    )(rows, group, trailing)


def onehot(slot, start, count):
    here = start + lax.broadcasted_iota(jnp.int32, (count, slot.shape[1]), 0)
    return jnp.where(here == slot, 1.0, 0.0).astype(jnp.bfloat16)


def pieces(a):
    hi, rest = split(a)
    mid, lo = split(a - hi.astype(jnp.float32))
    return hi, mid, lo


def owner_at(place):
    if place < NX * NEAR:
        x, y = divmod(place, NEAR)
    else:
        y, x = divmod(place, NX)
    return NX * y + x


def place_of(y, x):
    return jnp.where(y < NEAR, x * NEAR + y, NX * y + x)


def order_kernel(slot_ref, slots_ref, out_ref):
    owners, cols, _ = slots_ref.shape
    acc = None
    for g in range(owners // SHARE):
        part = slots_ref[owner_at(SHARE * g)]
        for i in range(1, SHARE):
            part = part + slots_ref[owner_at(SHARE * g + i)]
        three = jnp.concatenate(pieces(part), axis=0)
        got = dot(three, onehot(slot_ref[...], g * LANES, LANES), precision=None)
        acc = got if acc is None else acc + got
    rows = acc[:cols] + acc[cols : 2 * cols] + acc[2 * cols :]
    out_ref[...] = jnp.broadcast_to(rows[None], out_ref.shape)


def to_order(slots, slot):
    owners, cols, _ = slots.shape
    return pl.pallas_call(
        order_kernel,
        in_specs=[VMEM, VMEM],
        out_specs=VMEM,
        out_shape=jax.ShapeDtypeStruct((owners, cols, slot.shape[1]), jnp.float32),
        cost_estimate=pl.CostEstimate(flops=0, bytes_accessed=0, transcendentals=0),
        name="slots_to_order",
    )(slot, slots)


def tops_kernel(first_ref, slot_ref, trail_ref, *refs):
    blocks = NX + NY - NEAR
    outs, sems = refs[:blocks], refs[blocks]

    def run(top, rows):
        read = pltpu.make_async_copy(trail_ref.at[pl.ds(0, top.shape[0]), :], top, sems.at[blocks])
        read.start()
        read.wait()
        parts = pieces(top[...])
        writes = []
        start = 0
        for b, out in enumerate(outs):
            count = out.shape[0]
            pick = onehot(slot_ref[...], start, count)
            hi, mid, lo = (dot(pick, part, precision=None) for part in parts)
            rows[pl.ds(start, count), :] = hi + mid + lo
            writes.append(pltpu.make_async_copy(rows.at[pl.ds(start, count), :], out, sems.at[b]))
            writes[-1].start()
            start += count
        for copy in writes:
            copy.wait()

    @pl.when(first_ref[0] == 1)
    def _():
        n, cols = slot_ref.shape[1], trail_ref.shape[1]
        pl.run_scoped(
            run,
            pltpu.VMEM((n, cols), jnp.float32),
            pltpu.VMEM((NPROW * CAP, cols), jnp.float32),
        )


def to_owners(first, slot, trailing):
    cols = trailing.shape[1]
    hbm = pl.BlockSpec(memory_space=pltpu.HBM)
    counts = [NEAR * CAP] * NX + [NX * CAP] * (NY - NEAR)
    return pl.pallas_call(
        tops_kernel,
        in_specs=[SMEM, VMEM, pl.BlockSpec(memory_space=pl.ANY)],
        out_specs=[hbm] * len(counts),
        out_shape=[pltpu.HBM((count, cols), jnp.float32) for count in counts],
        scratch_shapes=[pltpu.SemaphoreType.DMA((len(counts) + 1,))],
        compiler_params=pltpu.CompilerParams(vmem_limit_bytes=24 * 1024 * 1024),
        cost_estimate=pl.CostEstimate(flops=20_000_000_000, bytes_accessed=0, transcendentals=0),
        name="tops_to_owners",
    )(first, slot, trailing)


def invert_upper(u_ref, m_ref, between):
    n = u_ref.shape[0]
    base = 128
    row = lax.broadcasted_iota(jnp.int32, (base, base), 0)
    col = lax.broadcasted_iota(jnp.int32, (base, base), 1)
    eye = jnp.where(row == col, 1.0, 0.0)
    blocks = [u_ref[pl.ds(b * base, base), pl.ds(b * base, base)] for b in range(n // base)]
    invs = [eye] * len(blocks)
    m_ref[...] = jnp.zeros_like(m_ref)
    s = 1
    while s < base:
        mask = (row // (2 * s) == col // (2 * s)) & (row % (2 * s) < s) & (col % (2 * s) >= s)
        parts = [jnp.where(mask, u, 0.0) for u in blocks]
        if s == 1:
            invs = [m - q for m, q in zip(invs, parts)]
        else:
            half = [dot(m, q) for m, q in zip(invs, parts)]
            invs = [m - dot(h, m) for m, h in zip(invs, half)]
        between(s)
        s *= 2
    for b, m in enumerate(invs):
        m_ref[pl.ds(b * base, base), pl.ds(b * base, base)] = m
    s = base
    while s < n:
        for b in range(0, n, 2 * s):
            up, dn = pl.ds(b, s), pl.ds(b + s, s)
            t = dot(m_ref[up, up], u_ref[up, dn])
            m_ref[up, dn] = -dot(t, m_ref[dn, dn])
        s *= 2


TILE = 256


def factor_kernel(full_ref, m3_ref, l2_ref, u, m, lt, m3, l2, sems):
    n, rows = lt.shape
    get_u = pltpu.make_async_copy(full_ref.at[:, pl.ds(rows, n)], u, sems.at[0])
    get_l = pltpu.make_async_copy(full_ref.at[:, pl.ds(0, rows)], lt, sems.at[1])
    get_u.start()
    get_u.wait()
    get_l.start()

    todo = list(range(rows // TILE))
    puts = []

    def between(s):
        if s < 4 or not todo:
            return
        i = todo.pop(0)
        if i == 0:
            get_l.wait()
        at = pl.ds(i * TILE, TILE)
        hi, lo = split(lt[:, at].T)
        l2[at, pl.ds(0, n)] = hi
        l2[at, pl.ds(n, n)] = lo
        puts.append(pltpu.make_async_copy(l2.at[at, :], l2_ref.at[at, :], sems.at[2 + i]))
        puts[-1].start()

    invert_upper(u, m, between)
    while todo:
        between(n)
    hi, lo = split(m[...])
    m3[pl.ds(0, n), :] = hi
    m3[pl.ds(n, n), :] = hi
    m3[pl.ds(2 * n, n), :] = lo
    puts.append(pltpu.make_async_copy(m3, m3_ref, sems.at[2 + rows // TILE]))
    puts[-1].start()
    for copy in puts:
        copy.wait()


def factor(full, rows):
    n = full.shape[0]
    f32, bf16 = jnp.float32, jnp.bfloat16
    hbm = pl.BlockSpec(memory_space=pl.ANY)
    return pl.pallas_call(
        factor_kernel,
        in_specs=[hbm],
        out_specs=[hbm, hbm],
        out_shape=[pltpu.HBM((3 * n, n), bf16), pltpu.HBM((rows, 2 * n), bf16)],
        scratch_shapes=[
            pltpu.VMEM((n, n), f32),
            pltpu.VMEM((n, n), f32),
            pltpu.VMEM((n, rows), f32),
            pltpu.VMEM((3 * n, n), bf16),
            pltpu.VMEM((rows, 2 * n), bf16),
            pltpu.SemaphoreType.DMA((3 + rows // TILE,)),
        ],
        compiler_params=pltpu.CompilerParams(vmem_limit_bytes=20 * 1024 * 1024),
        cost_estimate=pl.CostEstimate(flops=200_000_000_000, bytes_accessed=0, transcendentals=0),
        name="factor",
    )(pltpu.with_memory_space_constraint(full, pltpu.HBM))


def update_kernel(rows_ref, flags_ref, *refs):
    parts, refs = refs[:NEAR], refs[NEAR:]
    m3_ref, l2_ref, ct_ref, trail_ref, out_ref, m3, l2, ct, x3, here, top, sems = refs
    rows, n = l2.shape[0], ct.shape[1]
    tiles, late = rows // TILE, n // TILE
    sources = ((ct_ref, ct), (m3_ref, m3), (l2_ref, l2))
    gets = [pltpu.make_async_copy(a, b, sems.at[tiles + i]) for i, (a, b) in enumerate(sources)]
    for copy in gets:
        copy.start()
    received = parts[1][...]
    for part in parts[2:]:
        received = received + part[...]
    top[...] = jnp.where(flags_ref[1] == 1, parts[0][...], received)
    here[...] = trail_ref[...]
    for r in range(CAP):
        row = rows_ref[r]

        @pl.when(row >= 0)
        def _(r=r, row=row):
            here[pl.ds(row, 1), :] = top[pl.ds(r, 1), :]

    gets[0].wait()
    gets[1].wait()
    hi, lo = split(ct[...])
    xt = dot(jnp.concatenate([hi, lo, hi], axis=1), m3[...], precision=None)
    hi, lo = split(xt)
    x3[:, pl.ds(0, n)] = hi
    x3[:, pl.ds(n, n)] = hi
    x3[:, pl.ds(2 * n, n)] = lo

    gets[2].wait()
    puts = []

    def put(i):
        at = pl.ds(i * TILE, TILE)
        puts.append(pltpu.make_async_copy(here.at[at, :], out_ref.at[at, :], sems.at[i]))
        puts[-1].start()

    both = ((1,), (1,))
    for i in list(range(late, tiles)) + list(range(late)):
        at = pl.ds(i * TILE, TILE)
        acc = dot(l2[at, :], x3[:, pl.ds(0, 2 * n)], both, None)
        acc = acc + dot(l2[at, pl.ds(0, n)], x3[:, pl.ds(2 * n, n)], both, None)
        here[at, :] = here[at, :] - acc
        if i >= late:
            put(i)

    @pl.when(flags_ref[0] == 1)
    def _():
        here[pl.ds(0, n), :] = xt.T

    for i in range(late):
        put(i)
    for copy in puts:
        copy.wait()


def update(rows, flags, parts, m3, l2, ct, trailing):
    height, cols = trailing.shape
    n = ct.shape[1]
    hbm = pl.BlockSpec(memory_space=pl.ANY)
    f32, bf16 = jnp.float32, jnp.bfloat16
    return pl.pallas_call(
        update_kernel,
        in_specs=[SMEM, SMEM] + [VMEM] * len(parts) + [hbm] * 3 + [VMEM],
        out_specs=hbm,
        out_shape=jax.ShapeDtypeStruct(trailing.shape, f32),
        scratch_shapes=[
            pltpu.VMEM(m3.shape, bf16),
            pltpu.VMEM(l2.shape, bf16),
            pltpu.VMEM(ct.shape, f32),
            pltpu.VMEM((cols, 3 * n), bf16),
            pltpu.VMEM((height, cols), f32),
            pltpu.VMEM((CAP, cols), f32),
            pltpu.SemaphoreType.DMA((height // TILE + 4,)),
        ],
        compiler_params=pltpu.CompilerParams(vmem_limit_bytes=24 * 1024 * 1024),
        name="solve_update",
    )(rows, flags, *parts, *(pltpu.with_memory_space_constraint(a, pltpu.HBM) for a in (m3, l2)), ct, trailing)


def from_hubs(k):
    pairs = [(x, NX * k + x) for x in range(NX)]
    if k < NX:
        pairs += [(NX * y, NX * y + k) for y in range(NEAR, NY)]
    return pairs


def after(value, *others):
    return lax.optimization_barrier((value, *others))[0]


def on_device(trailing, l_panel, pivots):
    rows_here, cols_here = trailing.shape
    block = pivots.shape[0]
    p = lax.axis_index(PROW)
    first = (p == 0).astype(jnp.int32)[None]

    owner = pivots // rows_here
    local = pivots % rows_here
    ks = jnp.arange(block, dtype=jnp.int32)
    before = (owner[None, :] == owner[:, None]) & (ks[None, :] < ks[:, None])
    place = place_of(owner // NX, owner % NX)
    slot = place * CAP + jnp.sum(before.astype(jnp.int32), axis=1)
    y, x = lax.axis_index("y"), lax.axis_index("x")
    here = place_of(y, x)
    mine = slot[None, :] == (here * CAP + jnp.arange(CAP, dtype=jnp.int32))[:, None]
    rows = jnp.sum(jnp.where(mine, local[None, :] + 1, 0), axis=1) - 1
    hub = (y == 0) | ((y >= NEAR) & (x == 0))

    lt = l_panel.T
    slab = lt[:, :block]
    got = [lax.ppermute(slab, PROW, [(0, k)]) for k in range(1, NX)]
    slab = jnp.where(p == 0, slab, sum(got))
    lanes = pick(rows, (here % SHARE)[None], trailing)
    slab, lanes = lax.optimization_barrier((slab, lanes))
    got = [lax.ppermute(slab, PROW, [(x0, NX * k + x0) for x0 in range(NX)]) for k in range(1, NY)]
    slab = jnp.where(y == 0, slab, sum(got))

    tops = to_owners(first, slot[None, :], after(trailing, lanes))
    slab = after(slab, tops[1])

    full = lax.all_gather(jnp.concatenate([lt, slab], axis=1), PCOL, axis=0, tiled=True)

    near = [lax.ppermute(tops[k], PROW, [(0, k)]) for k in range(1, NX)]
    far = [lax.ppermute(tops[NX + i], PROW, [(0, NX * (NEAR + i))]) for i in range(NY - NEAR)]

    lanes = after(lanes, tops[1])
    share = lanes.reshape(NPROW, cols_here // NPROW, LANES)
    share = lax.all_to_all(share, PROW, 0, 0, tiled=True)

    ct = to_order(share, slot[None, :])
    near, far = lax.optimization_barrier((near, far, ct))[:2]
    ct = lax.all_to_all(ct, PROW, 0, 0, tiled=True).reshape(cols_here, block)

    near = jnp.where(p == 0, tops[0], sum(near)).reshape(NEAR, CAP, cols_here)
    far = sum(far).reshape(NX, CAP, cols_here)
    got = []
    for k in range(1, NEAR):
        sent = jnp.where(y == 0, near[k], far[k]) if k < NX else near[k]
        got.append(lax.ppermute(sent, PROW, from_hubs(k)))

    m3, l2 = factor(full, rows_here)
    got, m3 = lax.optimization_barrier((got, m3))
    own = jnp.where(y == 0, near[0], far[0])
    flags = jnp.stack([first[0], hub.astype(jnp.int32)])
    return update(rows, flags, [own] + got, m3, l2, ct, trailing)


def solution(mesh):
    grid = Mesh(mesh.devices.reshape(NY, NX, NZ, NC), ("y", "x", "z", "c"))
    placed = (P(PROW, PCOL), P(PROW, PCOL), P())
    return jax.shard_map(
        on_device, mesh=grid, in_specs=placed, out_specs=P(PROW, PCOL), check_vma=False
    )
```

```python
import jax
import jax.numpy as jnp
from jax import lax
from jax.experimental import pallas as pl
from jax.experimental.pallas import tpu as pltpu
from jax.sharding import Mesh, PartitionSpec as P

NX, NY, NZ, NC = 4, 8, 8, 2
NPROW = NX * NY
CAP = 32
LANES = 128
ORDER1 = (1, 2, 3, 4, 5, 6, 7)
ORDER2 = (4, 3, 2, 1, 5)
FARS = (6, 7)
NEARS = (0, 1, 2, 3, 4, 5)
NEAR = len(NEARS)
SHARE = LANES // CAP
PROW, PCOL = ("y", "x"), ("z", "c")
HI = lax.Precision.HIGHEST
SMEM = pl.BlockSpec(memory_space=pltpu.SMEM)
VMEM = pl.BlockSpec(memory_space=pltpu.VMEM)


def dot(a, b, dims=((1,), (0,)), precision=HI):
    return lax.dot_general(a, b, (dims, ((), ())), precision=precision, preferred_element_type=jnp.float32)


def split(a):
    hi = a.astype(jnp.bfloat16)
    lo = (a - hi.astype(jnp.float32)).astype(jnp.bfloat16)
    return hi, lo


def pick_kernel(rows_ref, group_ref, trail_ref, out_ref, near, picked, sem):
    here = [jnp.maximum(rows_ref[r], 0) for r in range(CAP)]
    for r in range(CAP):
        tile = pl.multiple_of((here[r] // 8) * 8, 8)
        pltpu.make_async_copy(trail_ref.at[pl.ds(tile, 8), :], near.at[r], sem).start()
    pltpu.make_async_copy(near, near, sem).wait()
    for r in range(CAP):
        picked[pl.ds(r, 1), :] = near[r, pl.ds(here[r] % 8, 1), :]
    parts = [jnp.where(group_ref[0] == g, picked[...], 0.0) for g in range(SHARE)]
    out_ref[...] = jnp.concatenate(parts, axis=0).T


def pick(rows, group, trailing):
    cols = trailing.shape[1]
    return pl.pallas_call(
        pick_kernel,
        in_specs=[SMEM, SMEM, pl.BlockSpec(memory_space=pl.ANY)],
        out_specs=VMEM,
        out_shape=jax.ShapeDtypeStruct((cols, LANES), jnp.float32),
        scratch_shapes=[
            pltpu.VMEM((CAP, 8, cols), jnp.float32),
            pltpu.VMEM((CAP, cols), jnp.float32),
            pltpu.SemaphoreType.DMA,
        ],
        cost_estimate=pl.CostEstimate(flops=0, bytes_accessed=0, transcendentals=0),
        name="pick_rows",
    )(rows, group, trailing)


def onehot(slot, start, count):
    here = start + lax.broadcasted_iota(jnp.int32, (count, slot.shape[1]), 0)
    return jnp.where(here == slot, 1.0, 0.0).astype(jnp.bfloat16)


def pieces(a):
    hi, rest = split(a)
    mid, lo = split(a - hi.astype(jnp.float32))
    return hi, mid, lo


def owner_at(place):
    if place < NX * NEAR:
        x, i = divmod(place, NEAR)
        y = NEARS[i]
    else:
        i, x = divmod(place - NX * NEAR, NX)
        y = FARS[i]
    return NX * y + x


def is_far(y):
    return (y >= FARS[0]) & (y <= FARS[-1])


def place_of(y, x):
    near = x * NEAR + jnp.where(y < FARS[0], y, y - len(FARS))
    return jnp.where(is_far(y), NX * NEAR + NX * (y - FARS[0]) + x, near)


def order_kernel(slot_ref, slots_ref, out_ref):
    owners, cols, _ = slots_ref.shape
    acc = None
    for g in range(owners // SHARE):
        part = slots_ref[owner_at(SHARE * g)]
        for i in range(1, SHARE):
            part = part + slots_ref[owner_at(SHARE * g + i)]
        three = jnp.concatenate(pieces(part), axis=0)
        got = dot(three, onehot(slot_ref[...], g * LANES, LANES), precision=None)
        acc = got if acc is None else acc + got
    rows = acc[:cols] + acc[cols : 2 * cols] + acc[2 * cols :]
    out_ref[...] = jnp.broadcast_to(rows[None], out_ref.shape)


def to_order(slots, slot):
    owners, cols, _ = slots.shape
    return pl.pallas_call(
        order_kernel,
        in_specs=[VMEM, VMEM],
        out_specs=VMEM,
        out_shape=jax.ShapeDtypeStruct((owners, cols, slot.shape[1]), jnp.float32),
        cost_estimate=pl.CostEstimate(flops=0, bytes_accessed=0, transcendentals=0),
        name="slots_to_order",
    )(slot, slots)


def tops_kernel(first_ref, slot_ref, trail_ref, *refs):
    blocks = NX + NY - NEAR
    outs, sems = refs[:blocks], refs[blocks]

    def run(top, rows):
        read = pltpu.make_async_copy(trail_ref.at[pl.ds(0, top.shape[0]), :], top, sems.at[blocks])
        read.start()
        read.wait()
        parts = pieces(top[...])
        writes = []
        start = 0
        for b, out in enumerate(outs):
            count = out.shape[0]
            pick = onehot(slot_ref[...], start, count)
            hi, mid, lo = (dot(pick, part, precision=None) for part in parts)
            rows[pl.ds(start, count), :] = hi + mid + lo
            writes.append(pltpu.make_async_copy(rows.at[pl.ds(start, count), :], out, sems.at[b]))
            writes[-1].start()
            start += count
        for copy in writes:
            copy.wait()

    @pl.when(first_ref[0] == 1)
    def _():
        n, cols = slot_ref.shape[1], trail_ref.shape[1]
        pl.run_scoped(
            run,
            pltpu.VMEM((n, cols), jnp.float32),
            pltpu.VMEM((NPROW * CAP, cols), jnp.float32),
        )


def to_owners(first, slot, trailing):
    cols = trailing.shape[1]
    hbm = pl.BlockSpec(memory_space=pltpu.HBM)
    counts = [NEAR * CAP] * NX + [NX * CAP] * (NY - NEAR)
    return pl.pallas_call(
        tops_kernel,
        in_specs=[SMEM, VMEM, pl.BlockSpec(memory_space=pl.ANY)],
        out_specs=[hbm] * len(counts),
        out_shape=[pltpu.HBM((count, cols), jnp.float32) for count in counts],
        scratch_shapes=[pltpu.SemaphoreType.DMA((len(counts) + 1,))],
        compiler_params=pltpu.CompilerParams(vmem_limit_bytes=24 * 1024 * 1024),
        cost_estimate=pl.CostEstimate(flops=20_000_000_000, bytes_accessed=0, transcendentals=0),
        name="tops_to_owners",
    )(first, slot, trailing)


def invert_upper(u_ref, m_ref, between):
    n = u_ref.shape[0]
    base = 128
    row = lax.broadcasted_iota(jnp.int32, (base, base), 0)
    col = lax.broadcasted_iota(jnp.int32, (base, base), 1)
    eye = jnp.where(row == col, 1.0, 0.0)
    blocks = [u_ref[pl.ds(b * base, base), pl.ds(b * base, base)] for b in range(n // base)]
    invs = [eye] * len(blocks)
    m_ref[...] = jnp.zeros_like(m_ref)
    s = 1
    while s < base:
        mask = (row // (2 * s) == col // (2 * s)) & (row % (2 * s) < s) & (col % (2 * s) >= s)
        parts = [jnp.where(mask, u, 0.0) for u in blocks]
        if s == 1:
            invs = [m - q for m, q in zip(invs, parts)]
        else:
            half = [dot(m, q) for m, q in zip(invs, parts)]
            invs = [m - dot(h, m) for m, h in zip(invs, half)]
        between(s)
        s *= 2
    for b, m in enumerate(invs):
        m_ref[pl.ds(b * base, base), pl.ds(b * base, base)] = m
    s = base
    while s < n:
        for b in range(0, n, 2 * s):
            up, dn = pl.ds(b, s), pl.ds(b + s, s)
            t = dot(m_ref[up, up], u_ref[up, dn])
            m_ref[up, dn] = -dot(t, m_ref[dn, dn])
        s *= 2


TILE = 256


def factor_kernel(full_ref, m2_ref, l2_ref, u, m, lt, m2, l2, sems):
    n, rows = lt.shape
    get_u = pltpu.make_async_copy(full_ref.at[:, pl.ds(rows, n)], u, sems.at[0])
    get_l = pltpu.make_async_copy(full_ref.at[:, pl.ds(0, rows)], lt, sems.at[1])
    get_u.start()
    get_u.wait()
    get_l.start()

    todo = list(range(rows // TILE))
    puts = []

    def between(s):
        if s < 4 or not todo:
            return
        i = todo.pop(0)
        if i == 0:
            get_l.wait()
        at = pl.ds(i * TILE, TILE)
        hi, lo = split(lt[:, at].T)
        l2[at, pl.ds(0, n)] = hi
        l2[at, pl.ds(n, n)] = lo
        puts.append(pltpu.make_async_copy(l2.at[at, :], l2_ref.at[at, :], sems.at[2 + i]))
        puts[-1].start()

    invert_upper(u, m, between)
    while todo:
        between(n)
    hi, lo = split(m[...])
    m2[pl.ds(0, n), :] = hi
    m2[pl.ds(n, n), :] = lo
    puts.append(pltpu.make_async_copy(m2, m2_ref, sems.at[2 + rows // TILE]))
    puts[-1].start()
    for copy in puts:
        copy.wait()


def factor(full, rows):
    n = full.shape[0]
    f32, bf16 = jnp.float32, jnp.bfloat16
    hbm = pl.BlockSpec(memory_space=pl.ANY)
    return pl.pallas_call(
        factor_kernel,
        in_specs=[hbm],
        out_specs=[hbm, hbm],
        out_shape=[pltpu.HBM((2 * n, n), bf16), pltpu.HBM((rows, 2 * n), bf16)],
        scratch_shapes=[
            pltpu.VMEM((n, n), f32),
            pltpu.VMEM((n, n), f32),
            pltpu.VMEM((n, rows), f32),
            pltpu.VMEM((2 * n, n), bf16),
            pltpu.VMEM((rows, 2 * n), bf16),
            pltpu.SemaphoreType.DMA((3 + rows // TILE,)),
        ],
        compiler_params=pltpu.CompilerParams(vmem_limit_bytes=20 * 1024 * 1024),
        cost_estimate=pl.CostEstimate(flops=200_000_000_000, bytes_accessed=0, transcendentals=0),
        name="factor",
    )(pltpu.with_memory_space_constraint(full, pltpu.HBM))


def update_kernel(rows_ref, flags_ref, *refs):
    parts, refs = refs[:NEAR], refs[NEAR:]
    m2_ref, l2_ref, ct, trail_ref, out_ref, m2, l2, x3, here, top, sems = refs
    rows, n = l2.shape[0], ct.shape[1]
    tiles, late = rows // TILE, n // TILE
    sources = ((m2_ref, m2), (l2_ref, l2))
    gets = [pltpu.make_async_copy(a, b, sems.at[tiles + i]) for i, (a, b) in enumerate(sources)]
    for copy in gets:
        copy.start()
    received = parts[1][...]
    for part in parts[2:]:
        received = received + part[...]
    top[...] = jnp.where(flags_ref[1] == 1, parts[0][...], received)
    here[...] = trail_ref[...]
    for r in range(CAP):
        row = rows_ref[r]

        @pl.when(row >= 0)
        def _(r=r, row=row):
            here[pl.ds(row, 1), :] = top[pl.ds(r, 1), :]

    hi, lo = split(ct[...])
    gets[0].wait()
    both = dot(jnp.concatenate([hi, lo], axis=0), m2[pl.ds(0, n), :], precision=None)
    xt = both[: ct.shape[0]] + (both[ct.shape[0] :] + dot(hi, m2[pl.ds(n, n), :], precision=None))
    hi, lo = split(xt)
    x3[:, pl.ds(0, n)] = hi
    x3[:, pl.ds(n, n)] = hi
    x3[:, pl.ds(2 * n, n)] = lo

    gets[1].wait()
    puts = []

    def put(i):
        at = pl.ds(i * TILE, TILE)
        puts.append(pltpu.make_async_copy(here.at[at, :], out_ref.at[at, :], sems.at[i]))
        puts[-1].start()

    both = ((1,), (1,))
    for i in list(range(late, tiles)) + list(range(late)):
        at = pl.ds(i * TILE, TILE)
        acc = dot(l2[at, :], x3[:, pl.ds(0, 2 * n)], both, None)
        acc = acc + dot(l2[at, pl.ds(0, n)], x3[:, pl.ds(2 * n, n)], both, None)
        here[at, :] = here[at, :] - acc
        if i >= late:
            put(i)

    @pl.when(flags_ref[0] == 1)
    def _():
        here[pl.ds(0, n), :] = xt.T

    for i in range(late):
        put(i)
    for copy in puts:
        copy.wait()


def update(rows, flags, parts, m2, l2, ct, trailing):
    height, cols = trailing.shape
    n = ct.shape[1]
    hbm = pl.BlockSpec(memory_space=pl.ANY)
    f32, bf16 = jnp.float32, jnp.bfloat16
    return pl.pallas_call(
        update_kernel,
        in_specs=[SMEM, SMEM] + [VMEM] * len(parts) + [hbm, hbm, VMEM, VMEM],
        out_specs=hbm,
        out_shape=jax.ShapeDtypeStruct(trailing.shape, f32),
        scratch_shapes=[
            pltpu.VMEM(m2.shape, bf16),
            pltpu.VMEM(l2.shape, bf16),
            pltpu.VMEM((cols, 3 * n), bf16),
            pltpu.VMEM((height, cols), f32),
            pltpu.VMEM((CAP, cols), f32),
            pltpu.SemaphoreType.DMA((height // TILE + 4,)),
        ],
        compiler_params=pltpu.CompilerParams(vmem_limit_bytes=24 * 1024 * 1024),
        name="solve_update",
    )(rows, flags, *parts, *(pltpu.with_memory_space_constraint(a, pltpu.HBM) for a in (m2, l2)), ct, trailing)


def from_hubs(k):
    pairs = [(x, NX * NEARS[k] + x) for x in range(NX)]
    if k < NX:
        pairs += [(NX * y, NX * y + k) for y in FARS]
    return pairs


def after(value, *others):
    return lax.optimization_barrier((value, *others))[0]


def on_device(trailing, l_panel, pivots):
    rows_here, cols_here = trailing.shape
    block = pivots.shape[0]
    p = lax.axis_index(PROW)
    first = (p == 0).astype(jnp.int32)[None]

    owner = pivots // rows_here
    local = pivots % rows_here
    ks = jnp.arange(block, dtype=jnp.int32)
    before = (owner[None, :] == owner[:, None]) & (ks[None, :] < ks[:, None])
    place = place_of(owner // NX, owner % NX)
    slot = place * CAP + jnp.sum(before.astype(jnp.int32), axis=1)
    y, x = lax.axis_index("y"), lax.axis_index("x")
    here = place_of(y, x)
    mine = slot[None, :] == (here * CAP + jnp.arange(CAP, dtype=jnp.int32))[:, None]
    rows = jnp.sum(jnp.where(mine, local[None, :] + 1, 0), axis=1) - 1
    hub = (y == 0) | (is_far(y) & (x == 0))

    lt = l_panel.T
    slab = lt[:, :block]
    got = [lax.ppermute(slab, PROW, [(0, k)]) for k in range(1, NX)]
    slab = jnp.where(p == 0, slab, sum(got))
    lanes = pick(rows, (here % SHARE)[None], trailing)
    slab, lanes = lax.optimization_barrier((slab, lanes))
    got = [lax.ppermute(slab, PROW, [(x0, NX * k + x0) for x0 in range(NX)]) for k in ORDER1]
    slab = jnp.where(y == 0, slab, sum(got))

    tops = to_owners(first, slot[None, :], after(trailing, lanes))
    slab = after(slab, tops[1])

    full = lax.all_gather(jnp.concatenate([lt, slab], axis=1), PCOL, axis=0, tiled=True)

    near = [lax.ppermute(tops[k], PROW, [(0, k)]) for k in range(1, NX)]
    far = [lax.ppermute(tops[NX + i], PROW, [(0, NX * f)]) for i, f in enumerate(FARS)]

    lanes = after(lanes, tops[1])
    share = lanes.reshape(NPROW, cols_here // NPROW, LANES)
    share = lax.all_to_all(share, PROW, 0, 0, tiled=True)

    ct = to_order(share, slot[None, :])
    near, far = lax.optimization_barrier((near, far, ct))[:2]
    ct = lax.all_to_all(ct, PROW, 0, 0, tiled=True).reshape(cols_here, block)

    near = jnp.where(p == 0, tops[0], sum(near)).reshape(NEAR, CAP, cols_here)
    far = sum(far).reshape(NX, CAP, cols_here)
    got = []
    for k in ORDER2:
        sent = jnp.where(y == 0, near[k], far[k]) if k < NX else near[k]
        got.append(lax.ppermute(sent, PROW, from_hubs(k)))

    m2, l2 = factor(full, rows_here)
    got, m2 = lax.optimization_barrier((got, m2))
    own = jnp.where(y == 0, near[0], far[0])
    flags = jnp.stack([first[0], hub.astype(jnp.int32)])
    return update(rows, flags, [own] + got, m2, l2, ct, trailing)


def solution(mesh):
    grid = Mesh(mesh.devices.reshape(NY, NX, NZ, NC), ("y", "x", "z", "c"))
    placed = (P(PROW, PCOL), P(PROW, PCOL), P())
    return jax.shard_map(
        on_device, mesh=grid, in_specs=placed, out_specs=P(PROW, PCOL), check_vma=False
    )
```
